32 devices in a mesh: dp: 32 (over z, y, x, core).
Axes of the slice: x: 2, y: 2, z: 4, core: 2. Of those that a mesh axis runs over, the one named last changes fastest.
Arguments:
- tokens: bfloat16 [16384, 1024], P('dp'), may hold values from -6 to 6
- cotangent: bfloat16 [16384, 1024], P('dp'), may hold values from -16 to 16
- route: int32 [32, 512], P('dp'), may hold values from 0 to 511, as said below
- lengths: int32 [64, 4], P('dp'), may hold values from 1 to 192, 256 in all within a row
- attn_gain: bfloat16 [1024], P('dp'), may hold values from 0.099609375 to 1.8984375
- w_query: bfloat16 [1024, 1024], P('dp'), may hold values from -0.1875 to 0.1875
- key_weight: bfloat16 [1024, 512], P('dp'), may hold values from -0.1875 to 0.1875
- value_weight: bfloat16 [1024, 512], P('dp'), may hold values from -0.1875 to 0.1875
- query_gain: bfloat16 [64], replicated, may hold values from 0.099609375 to 1.8984375
- key_norm_gain: bfloat16 [64], replicated, may hold values from 0.099609375 to 1.8984375
- w_out: bfloat16 [1024, 1024], P('dp'), may hold values from -1 to 1
- ffn_gain: bfloat16 [1024], P('dp'), may hold values from 0.099609375 to 1.8984375
- w_gate: bfloat16 [1024, 4608], P('dp'), may hold values from -0.1875 to 0.1875
- w_up: bfloat16 [1024, 4608], P('dp'), may hold values from -0.1875 to 0.1875
- w_down: bfloat16 [4608, 1024], P('dp'), may hold values from -0.09375 to 0.09375
Outputs:
- output: bfloat16 [16384, 1024], P('dp')
- input_grad: bfloat16 [16384, 1024], P('dp')
- grad_attn_gain: float32 [1024], P('dp')
- grad_query: float32 [1024, 1024], P('dp')
- grad_key: float32 [1024, 512], P('dp')
- grad_value: float32 [1024, 512], P('dp')
- grad_query_gain: float32 [64], replicated
- grad_key_gain: float32 [64], replicated
- grad_out: float32 [1024, 1024], P('dp')
- grad_ffn_gain: float32 [1024], P('dp')
- grad_gate: float32 [1024, 4608], P('dp')
- grad_up: float32 [1024, 4608], P('dp')
- grad_down: float32 [4608, 1024], P('dp')
The draws below stay inside these ranges and needn't reach their ends.
Inputs may be any that keep to these rules, and one draw needn't show every extreme that they name: Each row of route holds every number from 0 to 511 once.
All inputs are finite; a program needn't handle non-finite values.
Results may differ from the reference program's by a relative error of at most 0.013.
Values may be sent and summed in bfloat16 or wider, within the bound.
No kernel may reach another device: no remote copies, remote signals or barrier semaphores. Data moves between devices by JAX's collectives and lax.ppermute only.
A program may use at most 256 MiB of HBM per device.

```python
import math
import jax
import jax.numpy as jnp
import numpy as np
from jax import lax

MODEL_WIDTH = 1024
QUERY_HEADS = 16
KEY_VALUE_HEADS = 8
HEAD_SIZE = 64
FF = 4608
WINDOW_TOKENS = 256
MICRO = 2
NSEQ = 4
WINDOWS = 64
TOKENS = 16384
N_DP = 32


def shared_orders(key):
    row_count = MICRO * WINDOW_TOKENS
    keys_all = jax.random.split(key, N_DP)
    return jax.vmap(lambda single: jax.random.permutation(single, row_count))(keys_all).astype(jnp.int32)


def draw_route(key, part):
    orders = shared_orders(key)
    return orders


def draw_cotangent(key, part):
    orders = shared_orders(key)
    key = jax.random.fold_in(key, 7)
    share_rows = WINDOW_TOKENS // N_DP
    where_rows = jnp.argsort(orders, axis=1)
    target = where_rows % WINDOW_TOKENS // share_rows
    factor = 1.0 + 2.0 * target.astype(jnp.float32) / (N_DP - 1)
    factor = factor.reshape(TOKENS, 1)
    values = jnp.clip(jax.random.normal(key, (TOKENS, MODEL_WIDTH), jnp.float32), -4.0, 4.0) * factor
    return values.astype(jnp.bfloat16)


def shard_levels(key, dims, cuts, least, high):
    factor_of = 1.0
    for axis_at, shards_of in cuts:
        draws = jax.random.uniform(jax.random.fold_in(jax.random.fold_in(key, 6), axis_at), (shards_of,), jnp.float32, least / len(cuts), high / len(cuts))
        factor_of = factor_of * jnp.repeat(jnp.exp(draws), dims[axis_at] // shards_of).reshape((-1,) + (1,) * (len(dims) - 1 - axis_at))
    return factor_of


def split_up(count, total, bound, slope):
    portions = [(1 << 20) // math.isqrt(grade ** slope) + 1 for grade in range(2, count + 1)]
    surplus, holding = total - bound - (count - 1), [1] * (count - 1)
    while surplus > 0:
        movable = [i for i in range(count - 1) if holding[i] < bound]
        pool, budget = sum([portions[i] for i in movable]), surplus
        for i in movable:
            addition = min(bound - holding[i], max(1, budget * portions[i] // pool), surplus)
            holding[i] = holding[i] + addition
            surplus = surplus - addition
    return np.array([bound] + holding)


def ragged_sizes(rng, amount, total, limit, lean):
    if amount == 2:
        one = jax.random.randint(rng, (), max(1, total - limit), min(limit, total - 1) + 1)
        return jnp.stack([one, total - one])
    sizes = jnp.asarray(split_up(amount, total, limit, lean), jnp.int32)
    pairs = (amount - 1) // 2
    giver, taker = sizes[1:1 + 2 * pairs:2], sizes[2:2 + 2 * pairs:2]
    room = jnp.minimum(giver - 1, limit - taker)
    shifted = jax.random.randint(jax.random.fold_in(rng, 1), (pairs,), 0, 1 << 20) % (room + 1)
    sizes = sizes.at[1:1 + 2 * pairs:2].set(giver - shifted).at[2:2 + 2 * pairs:2].set(taker + shifted)
    return sizes[jax.random.permutation(jax.random.fold_in(rng, 2), amount)]


def scatter_about(stream_key, extent, spread, bound, shards=(), kind=jnp.bfloat16):
    drawn = jax.random.normal(stream_key, extent, jnp.float32) * spread
    if len(shards) > 0:
        drawn = shard_levels(stream_key, extent, shards, -0.22, 0.18) * drawn
    return jnp.clip(drawn, min=-bound, max=bound).astype(kind)


def setup_inputs(seed: int = 0) -> dict:
    arg_keys = jax.random.split(jax.random.key(seed), 16)
    tokens = scatter_about(arg_keys[0], (TOKENS, MODEL_WIDTH), 1.0, 6.0, ((0, 32),))
    cotangent = draw_cotangent(jax.random.fold_in(arg_keys[15], 71), 0)
    route = draw_route(jax.random.fold_in(arg_keys[15], 71), 0)
    lengths = jax.vmap(lambda own: ragged_sizes(own, NSEQ, WINDOW_TOKENS, 3 * WINDOW_TOKENS // 4, 2))(jax.random.split(arg_keys[3], WINDOWS)).reshape((WINDOWS, NSEQ)).astype(jnp.int32)
    attn_gain = jnp.clip(1.0 + 0.18 * jax.random.normal(arg_keys[4], (MODEL_WIDTH,), jnp.float32), 0.099609375, 1.8984375).astype(jnp.bfloat16)
    w_query = scatter_about(arg_keys[5], (MODEL_WIDTH, QUERY_HEADS * HEAD_SIZE), MODEL_WIDTH ** -0.5, 0.1875, ((0, 32),))
    key_weight = scatter_about(arg_keys[6], (MODEL_WIDTH, KEY_VALUE_HEADS * HEAD_SIZE), MODEL_WIDTH ** -0.5, 0.1875, ((0, 32),))
    value_weight = scatter_about(arg_keys[7], (MODEL_WIDTH, KEY_VALUE_HEADS * HEAD_SIZE), MODEL_WIDTH ** -0.5, 0.1875, ((0, 32),))
    query_gain = jnp.clip(1.0 + 0.18 * jax.random.normal(arg_keys[8], (HEAD_SIZE,), jnp.float32), 0.099609375, 1.8984375).astype(jnp.bfloat16)
    key_norm_gain = jnp.clip(1.0 + 0.18 * jax.random.normal(arg_keys[9], (HEAD_SIZE,), jnp.float32), 0.099609375, 1.8984375).astype(jnp.bfloat16)
    w_out = scatter_about(arg_keys[10], (QUERY_HEADS * HEAD_SIZE, MODEL_WIDTH), (QUERY_HEADS * HEAD_SIZE // 32) ** -0.5, 1.0, ((0, 32),))
    ffn_gain = jnp.clip(1.0 + 0.18 * jax.random.normal(arg_keys[11], (MODEL_WIDTH,), jnp.float32), 0.099609375, 1.8984375).astype(jnp.bfloat16)
    w_gate = scatter_about(arg_keys[12], (MODEL_WIDTH, FF), MODEL_WIDTH ** -0.5, 0.1875, ((0, 32),))
    w_up = scatter_about(arg_keys[13], (MODEL_WIDTH, FF), MODEL_WIDTH ** -0.5, 0.1875, ((0, 32),))
    w_down = scatter_about(arg_keys[14], (FF, MODEL_WIDTH), FF ** -0.5, 0.09375, ((0, 32),))
    return {"tokens": tokens, "cotangent": cotangent, "route": route, "lengths": lengths, "attn_gain": attn_gain, "w_query": w_query, "key_weight": key_weight, "value_weight": value_weight, "query_gain": query_gain, "key_norm_gain": key_norm_gain, "w_out": w_out, "ffn_gain": ffn_gain, "w_gate": w_gate, "w_up": w_up, "w_down": w_down}


EPS = 1e-05
THETA = 1000000.0
NEGATIVE = -1e+30

@jax.custom_vjp
def reduced_precision(v):
    return lax.optimization_barrier(v.astype(jnp.bfloat16)).astype(jnp.float32)

@jax.custom_vjp
def low_back(v):
    return v

def low_keep(v):
    return (reduced_precision(v), None)

def low_pass(kept, grad):
    return (grad,)

def back_keep(v):
    return (v, None)

def back_low(kept, grad):
    return (reduced_precision(grad),)
reduced_precision.defvjp(low_keep, low_pass)
low_back.defvjp(back_keep, back_low)

def product(left, right):
    return jnp.dot(left, right, precision=lax.Precision.HIGHEST, preferred_element_type=jnp.float32)

def root_mean_scale(values, gain):
    return values * lax.rsqrt(lax.optimization_barrier(jnp.mean(values * values, axis=-1, keepdims=True)) + EPS) * gain

def tables(positions, half_dim):
    steps_index = jnp.arange(half_dim, dtype=jnp.float32)
    inverse_freq = THETA ** (-steps_index / half_dim)
    angles = positions.astype(jnp.float32)[:, None] * inverse_freq[None, :]
    return (jnp.cos(angles), jnp.sin(angles))

def rotate_halves(values, cosine_table, sine_table):
    half_dim = values.shape[-1] // 2
    lower_half = values[..., :half_dim]
    upper_half = values[..., half_dim:]
    return jnp.concatenate([lower_half * cosine_table - upper_half * sine_table, upper_half * cosine_table + lower_half * sine_table], axis=-1)

def layout(lengths_row):
    places = jnp.arange(WINDOW_TOKENS, dtype=jnp.int32)
    ends = jnp.cumsum(lengths_row).astype(jnp.int32)
    segment = lax.optimization_barrier(jnp.sum((places[:, None] >= ends[None, :]).astype(jnp.int32), axis=1)).astype(jnp.int32)
    starts = (ends - lengths_row).astype(jnp.int32)
    picked = segment[:, None] == jnp.arange(NSEQ, dtype=jnp.int32)[None, :]
    begins = lax.optimization_barrier(jnp.sum(jnp.where(picked, starts[None, :], 0), axis=1)).astype(jnp.int32)
    return (segment, (places - begins).astype(jnp.int32))

def window_attend(blocks):
    query_matrix, key_matrix, value_matrix, segment = blocks
    places = jnp.arange(WINDOW_TOKENS, dtype=jnp.int32)
    allowed = (segment[:, None] == segment[None, :]) & (places[None, :] <= places[:, None])
    grouped_queries = query_matrix.reshape(WINDOW_TOKENS, KEY_VALUE_HEADS, QUERY_HEADS // KEY_VALUE_HEADS, HEAD_SIZE)
    scores = jnp.einsum('qkrd,tkd->krqt', grouped_queries, key_matrix, precision=lax.Precision.HIGHEST) * HEAD_SIZE ** (-0.5)
    scores = low_back(scores)
    scores = jnp.where(allowed[None, None], scores, NEGATIVE)
    probs = jax.nn.softmax(scores, axis=-1)
    head_mixture = jnp.einsum('krqt,tkd->qkrd', reduced_precision(probs), value_matrix, precision=lax.Precision.HIGHEST)
    return head_mixture.reshape(WINDOW_TOKENS, QUERY_HEADS * HEAD_SIZE)

def forward(params, window_inputs, segment_labels, positions):
    attn_gain, w_query, key_weight, value_weight, query_gain, key_norm_gain, w_out, ffn_gain, w_gate, w_up, w_down = params
    shift_amount = window_inputs.shape[0]
    rows_flat = window_inputs.reshape(shift_amount * WINDOW_TOKENS, MODEL_WIDTH)
    normed = reduced_precision(root_mean_scale(rows_flat, attn_gain))
    query_proj = low_back(product(normed, w_query))
    key_projected = low_back(product(normed, key_weight))
    value_matrix = reduced_precision(low_back(product(normed, value_weight)))
    cosine_table, sine_table = tables(positions.reshape(shift_amount * WINDOW_TOKENS), HEAD_SIZE // 2)
    cosine_table = cosine_table[:, None, :]
    sine_table = sine_table[:, None, :]
    query_matrix = reduced_precision(rotate_halves(root_mean_scale(query_proj.reshape(shift_amount * WINDOW_TOKENS, QUERY_HEADS, HEAD_SIZE), query_gain), cosine_table, sine_table))
    key_matrix = reduced_precision(rotate_halves(root_mean_scale(key_projected.reshape(shift_amount * WINDOW_TOKENS, KEY_VALUE_HEADS, HEAD_SIZE), key_norm_gain), cosine_table, sine_table))
    head_mixture = lax.map(jax.checkpoint(window_attend), (query_matrix.reshape(shift_amount, WINDOW_TOKENS, QUERY_HEADS, HEAD_SIZE), key_matrix.reshape(shift_amount, WINDOW_TOKENS, KEY_VALUE_HEADS, HEAD_SIZE), value_matrix.reshape(shift_amount, WINDOW_TOKENS, KEY_VALUE_HEADS, HEAD_SIZE), segment_labels))
    attended = reduced_precision(low_back(head_mixture.reshape(shift_amount * WINDOW_TOKENS, QUERY_HEADS * HEAD_SIZE)))
    resid = rows_flat + low_back(product(attended, w_out))
    normed_two = reduced_precision(root_mean_scale(resid, ffn_gain))
    gate_proj = low_back(product(normed_two, w_gate))
    up_proj = low_back(product(normed_two, w_up))
    hidden = reduced_precision(jax.nn.silu(gate_proj) * up_proj)
    return (resid + product(hidden, w_down)).reshape(shift_amount, WINDOW_TOKENS, MODEL_WIDTH)

def reference(tokens, cotangent, route, lengths, attn_gain, w_query, key_weight, value_weight, query_gain, key_norm_gain, w_out, ffn_gain, w_gate, w_up, w_down):
    share_rows = WINDOW_TOKENS // N_DP
    row_count = MICRO * WINDOW_TOKENS
    windows = MICRO * N_DP
    sources = (jnp.arange(N_DP, dtype=jnp.int32) * row_count)[:, None, None, None]
    picked = route.astype(jnp.int32).reshape(N_DP, MICRO, N_DP, share_rows) + sources
    picked = jnp.transpose(picked, (1, 2, 0, 3)).reshape(windows, WINDOW_TOKENS).astype(jnp.int32)
    window_lengths = jnp.transpose(lengths.reshape(N_DP, MICRO, NSEQ), (1, 0, 2)).reshape(windows, NSEQ)
    segment_labels, positions = jax.vmap(layout)(window_lengths)
    inputs = tokens.astype(jnp.float32)[picked]
    grads_in = cotangent.astype(jnp.float32)[picked]
    params = tuple((weight.astype(jnp.float32) for weight in (attn_gain, w_query, key_weight, value_weight, query_gain, key_norm_gain, w_out, ffn_gain, w_gate, w_up, w_down)))
    groups = windows // 8

    def scan_step(running, blocks):
        part_inputs, part_grads, part_segments, part_positions = blocks

        def apply(weights, values):
            return forward(weights, values, part_segments, part_positions)
        result, pull = jax.vjp(apply, params, part_inputs)
        weight_grads, input_grads = pull(part_grads)
        running = tuple((earlier + later for earlier, later in zip(running, weight_grads)))
        return (running, (result.astype(jnp.bfloat16), input_grads.astype(jnp.bfloat16)))
    start = tuple((jnp.zeros_like(weight) for weight in params))
    totals, (results, input_grads) = lax.scan(scan_step, start, (inputs.reshape(groups, 8, WINDOW_TOKENS, MODEL_WIDTH), grads_in.reshape(groups, 8, WINDOW_TOKENS, MODEL_WIDTH), segment_labels.reshape(groups, 8, WINDOW_TOKENS), positions.reshape(groups, 8, WINDOW_TOKENS)))
    flat_rows = picked.reshape(-1)
    output = jnp.zeros((TOKENS, MODEL_WIDTH), jnp.bfloat16).at[flat_rows].set(results.reshape(-1, MODEL_WIDTH))
    input_grad = jnp.zeros((TOKENS, MODEL_WIDTH), jnp.bfloat16).at[flat_rows].set(input_grads.reshape(-1, MODEL_WIDTH))
    return (output, input_grad, totals[0], totals[1], totals[2], totals[3], totals[4], totals[5], totals[6], totals[7], totals[8], totals[9], totals[10])
```

```python
from functools import partial

import jax
import jax.numpy as jnp
from jax import lax
from jax.experimental import pallas as pl
from jax.experimental.pallas import tpu as pltpu
from jax.sharding import PartitionSpec as P

QUERY_HEADS = 16
KEY_VALUE_HEADS = 8
HEAD_SIZE = 64
WINDOW_TOKENS = 256
MICRO = 2


EPS = 1e-05
THETA = 1000000.0
NEGATIVE = -1e30


def tdot(left, right):
    return lax.dot_general(
        left, right, (((0,), (0,)), ((), ())), preferred_element_type=jnp.float32
    )


def ntdot(left, right):
    return lax.dot_general(
        left, right, (((1,), (1,)), ((), ())), preferred_element_type=jnp.float32
    )


def norm_rows(values, gain):
    inverse = lax.rsqrt(jnp.mean(values * values, axis=-1, keepdims=True) + EPS)
    return (values * inverse * gain, inverse)


def norm_back(grad, values, inverse, gain):
    scaled = grad * gain
    grad_values = inverse * scaled - values * inverse * inverse * inverse * jnp.mean(
        scaled * values, axis=-1, keepdims=True
    )
    return (grad_values, grad * values * inverse)


def tables(positions, half_dim):
    steps_index = jnp.arange(half_dim, dtype=jnp.float32)
    inverse_freq = THETA ** (-steps_index / half_dim)
    angles = positions.astype(jnp.float32)[:, None] * inverse_freq[None, :]
    return (jnp.cos(angles), jnp.sin(angles))


def rotate_halves(values, cosine_table, sine_table, direction):
    half_dim = values.shape[-1] // 2
    lower_half = values[..., :half_dim]
    upper_half = values[..., half_dim:]
    return jnp.concatenate(
        [
            lower_half * cosine_table - direction * upper_half * sine_table,
            upper_half * cosine_table + direction * lower_half * sine_table,
        ],
        axis=-1,
    )


def layout(lengths_row, feature_width):
    places = jnp.arange(feature_width, dtype=jnp.int32)
    ends = jnp.cumsum(lengths_row)
    segment = jnp.sum((places[:, None] >= ends[None, :]).astype(jnp.int32), axis=1)
    starts = ends - lengths_row
    picked = segment[:, None] == jnp.arange(lengths_row.shape[0], dtype=jnp.int32)[None, :]
    begins = jnp.sum(jnp.where(picked, starts[None, :], 0), axis=1)
    allowed = (segment[:, None] == segment[None, :]) & (places[None, :] <= places[:, None])
    return (places - begins, allowed)


def masked_scores(allowed, query_block, key_block):
    factor = query_block.shape[-1] ** (-0.5)
    scores = (
        jnp.einsum("qrd,td->rqt", query_block, key_block, preferred_element_type=jnp.float32)
        * factor
    )
    return jnp.where(allowed[None], scores, NEGATIVE)


def attend_forward(allowed, blocks):
    query_block, key_block, value_block = blocks
    scores = masked_scores(allowed, query_block, key_block)
    row_max = jnp.max(scores, axis=-1, keepdims=True)
    exponent = jnp.exp(scores - row_max)
    totals = jnp.sum(exponent, axis=-1, keepdims=True)
    rounded_probs = (exponent / totals).astype(jnp.bfloat16)
    head_mixture = jnp.einsum(
        "rqt,td->qrd", rounded_probs, value_block, preferred_element_type=jnp.float32
    )
    return (head_mixture, (row_max + jnp.log(totals))[..., 0])


def attend_backward(allowed, blocks):
    query_block, key_block, value_block, grad_block, log_totals = blocks
    factor = query_block.shape[-1] ** (-0.5)
    scores = masked_scores(allowed, query_block, key_block)
    probs = jnp.exp(scores - log_totals[..., None])
    rounded_probs = probs.astype(jnp.bfloat16)
    grad_probs = jnp.einsum(
        "qrd,td->rqt", grad_block, value_block, preferred_element_type=jnp.float32
    )
    grad_value = jnp.einsum(
        "rqt,qrd->td", rounded_probs, grad_block, preferred_element_type=jnp.float32
    )
    inner = jnp.sum(probs * grad_probs, axis=-1, keepdims=True)
    grad_scores = (probs * (grad_probs - inner)).astype(jnp.bfloat16)
    grad_query = (
        jnp.einsum("rqt,td->qrd", grad_scores, key_block, preferred_element_type=jnp.float32)
        * factor
    )
    grad_key = (
        jnp.einsum("rqt,qrd->td", grad_scores, query_block, preferred_element_type=jnp.float32)
        * factor
    )
    return (grad_query, grad_key, grad_value)


def hop(values, bit, count):
    return lax.ppermute(values, "dp", [(i, i ^ (1 << bit)) for i in range(count)])


def owner_select(place, order, count, width):
    share = width // count
    bits = len(order)
    column = jnp.arange(width, dtype=jnp.int32)
    block = column // share
    mask = jnp.zeros_like(block)
    for at, bit in enumerate(order):
        mask = mask | (((block >> (bits - 1 - at)) & 1) << bit)
    feature = (place ^ mask) * share + column % share
    return (jnp.arange(width, dtype=jnp.int32)[:, None] == feature[None, :]).astype(jnp.bfloat16)


def select_rows(select, values):
    return lax.dot_general(
        select, values, (((0,), (1,)), ((), ())), preferred_element_type=jnp.float32
    ).astype(jnp.bfloat16)


def scatter_rest(kept, received, order, count):
    for bit in order:
        half = kept.shape[0] // 2
        sent = (kept[half:].astype(jnp.float32) + received[half:].astype(jnp.float32)).astype(jnp.bfloat16)
        kept = (kept[:half].astype(jnp.float32) + received[:half].astype(jnp.float32)).astype(jnp.bfloat16)
        received = hop(sent, bit, count)
    return kept.astype(jnp.float32) + received.astype(jnp.float32)


def product_scatter(parts, right, order, count):
    dot = lambda left: jnp.dot(left, right, preferred_element_type=jnp.float32)
    quarter = parts[0].shape[0]
    first = jnp.concatenate([dot(parts[2]).astype(jnp.bfloat16), dot(parts[3]).astype(jnp.bfloat16)], axis=0)
    got = hop(first, order[0], count)
    second = (dot(parts[1]) + got[quarter:].astype(jnp.float32)).astype(jnp.bfloat16)
    received = hop(second, order[1], count)
    kept = (dot(parts[0]) + got[:quarter].astype(jnp.float32)).astype(jnp.bfloat16)
    return scatter_rest(kept, received, order[2:], count)


def quarters(values):
    rows = values.shape[0] // 4
    return [values[i * rows : (i + 1) * rows] for i in range(4)]


def forward_kernel(n2_ref, gate_ref, up_ref, gp_ref, up_out_ref, hid_ref):
    n2 = n2_ref[...]
    gate = jnp.dot(n2, gate_ref[...], preferred_element_type=jnp.float32)
    up = jnp.dot(n2, up_ref[...], preferred_element_type=jnp.float32)
    hidden = gate * jax.nn.sigmoid(gate) * up
    gp_ref[...] = gate.astype(jnp.bfloat16)
    up_out_ref[...] = up.astype(jnp.bfloat16)
    hid_ref[...] = hidden.T.astype(jnp.bfloat16)


def ffn_forward(normed, weight):
    rows, width = normed.shape
    hidden = weight.shape[1] // 2
    tile = 512
    steps = hidden // tile
    shape = jax.ShapeDtypeStruct((rows, hidden), jnp.bfloat16)
    return pl.pallas_call(
        forward_kernel,
        grid=(steps,),
        in_specs=[
            pl.BlockSpec((rows, width), lambda j: (0, 0)),
            pl.BlockSpec((width, tile), lambda j: (0, j)),
            pl.BlockSpec((width, tile), lambda j: (0, j + steps)),
        ],
        out_specs=[
            pl.BlockSpec((rows, tile), lambda j: (0, j)),
            pl.BlockSpec((rows, tile), lambda j: (0, j)),
            pl.BlockSpec((tile, rows), lambda j: (j, 0)),
        ],
        out_shape=[shape, shape, jax.ShapeDtypeStruct((hidden, rows), jnp.bfloat16)],
        compiler_params=pltpu.CompilerParams(vmem_limit_bytes=48 << 20),
        cost_estimate=pl.CostEstimate(
            flops=4 * rows * width * hidden, bytes_accessed=4 * width * hidden + 6 * rows * hidden, transcendentals=rows * hidden
        ),
    )(normed, weight, weight)


def backward_kernel(gp_ref, up_ref, dy_ref, h1_ref, gate_ref, upw_ref, down_ref, dg_ref, du_ref, y_ref, dn_ref, acc_y, acc_n):
    j = pl.program_id(0)

    @pl.when(j == 0)
    def _():
        acc_y[...] = h1_ref[...]
        acc_n[...] = jnp.zeros_like(acc_n)

    gate = gp_ref[...].astype(jnp.float32)
    up = up_ref[...].astype(jnp.float32)
    down = down_ref[...]
    dhid = lax.dot_general(dy_ref[...], down, (((1,), (1,)), ((), ())), preferred_element_type=jnp.float32)
    sig = jax.nn.sigmoid(gate)
    silu = gate * sig
    dgate = (dhid * up * (sig + silu * (1.0 - sig))).astype(jnp.bfloat16)
    dup = (dhid * silu).astype(jnp.bfloat16)
    dg_ref[...] = dgate
    du_ref[...] = dup
    acc_y[...] += jnp.dot((silu * up).astype(jnp.bfloat16), down, preferred_element_type=jnp.float32)
    acc_n[...] += ntdot(dgate, gate_ref[...]) + ntdot(dup, upw_ref[...])

    @pl.when(j == pl.num_programs(0) - 1)
    def _():
        y_ref[...] = acc_y[...].astype(jnp.bfloat16)
        dn_ref[...] = acc_n[...]


def ffn_backward(gate, up, grads, resid, weight, down):
    rows, hidden = gate.shape
    width = grads.shape[1]
    tile = 512
    steps = hidden // tile
    shape = jax.ShapeDtypeStruct((rows, hidden), jnp.bfloat16)
    whole = pl.BlockSpec((rows, width), lambda j: (0, 0))
    cut = pl.BlockSpec((rows, tile), lambda j: (0, j))
    return pl.pallas_call(
        backward_kernel,
        grid=(steps,),
        in_specs=[
            cut,
            cut,
            whole,
            whole,
            pl.BlockSpec((width, tile), lambda j: (0, j)),
            pl.BlockSpec((width, tile), lambda j: (0, j + steps)),
            pl.BlockSpec((tile, width), lambda j: (j, 0)),
        ],
        out_specs=[cut, cut, whole, whole],
        out_shape=[
            shape,
            shape,
            jax.ShapeDtypeStruct((rows, width), jnp.bfloat16),
            jax.ShapeDtypeStruct((rows, width), jnp.float32),
        ],
        scratch_shapes=[pltpu.VMEM((rows, width), jnp.float32), pltpu.VMEM((rows, width), jnp.float32)],
        compiler_params=pltpu.CompilerParams(vmem_limit_bytes=56 << 20),
        cost_estimate=pl.CostEstimate(
            flops=8 * rows * width * hidden, bytes_accessed=6 * width * hidden + 8 * rows * hidden, transcendentals=rows * hidden
        ),
    )(gate, up, grads, resid, weight, weight, down)


def gather(values):
    return lax.all_gather(values, "dp", axis=0, tiled=True)


def per_device(
    tokens,
    cotangent,
    route,
    lengths,
    attn_gain,
    w_query,
    key_weight,
    value_weight,
    query_gain,
    key_norm_gain,
    w_out,
    ffn_gain,
    w_gate,
    w_up,
    w_down,
):
    f32 = jnp.float32
    low = jnp.bfloat16
    count = lax.axis_size("dp")
    levels = count.bit_length() - 1
    place = lax.axis_index("dp")
    window = WINDOW_TOKENS
    share = window // count
    width = tokens.shape[1]
    share_width = width // count
    q_width = QUERY_HEADS * HEAD_SIZE
    k_width = KEY_VALUE_HEADS * HEAD_SIZE
    rows = MICRO * window
    plain = list(range(levels))
    turned = [0, 2, 1] + list(range(3, levels))

    orders = route[0].reshape(MICRO, count, share).transpose(1, 0, 2).reshape(rows)
    deal = (orders[:, None] == jnp.arange(rows, dtype=jnp.int32)[None, :]).astype(low)

    def exchange(values):
        return lax.all_to_all(values, "dp", split_axis=0, concat_axis=0, tiled=True)

    def to_windows(values):
        sent = jnp.dot(deal, values, preferred_element_type=f32).astype(low)
        got = exchange(sent).reshape(count, MICRO, share, width)
        return got.transpose(1, 0, 2, 3).reshape(rows, width)

    def from_windows(values):
        sent = values.reshape(MICRO, count, share, width).transpose(1, 0, 2, 3).reshape(rows, width)
        return tdot(deal, exchange(sent)).astype(low)

    gains = jnp.pad(jnp.stack([attn_gain, ffn_gain], axis=1), ((0, 0), (0, 126)))
    attn_all = gather(jnp.concatenate([w_query, key_weight, value_weight, w_out, gains], axis=1))
    gate_up_all = gather(jnp.concatenate([w_gate, w_up], axis=1))
    down_all = gather(w_down)
    qkv_all = attn_all[:, : q_width + 2 * k_width]
    out_all = attn_all[:, q_width + 2 * k_width : q_width + 2 * k_width + width]
    gain_columns = attn_all[:, q_width + 2 * k_width + width :].astype(f32)
    attn_gain_all = gain_columns[:, 0]
    ffn_gain_all = gain_columns[:, 1]

    window_tokens = to_windows(tokens)
    window_grads = to_windows(cotangent)

    inputs = window_tokens.astype(f32)
    normed, inverse_one = norm_rows(inputs, attn_gain_all)
    normed_low = normed.astype(low)
    proj = jnp.dot(normed_low, qkv_all, preferred_element_type=f32)
    q_gain = query_gain.astype(f32)
    k_gain = key_norm_gain.astype(f32)
    query_proj = proj[:, :q_width].reshape(rows, QUERY_HEADS, HEAD_SIZE)
    key_proj = proj[:, q_width : q_width + k_width].reshape(rows, KEY_VALUE_HEADS, HEAD_SIZE)
    value_low = proj[:, q_width + k_width :].astype(low).reshape(rows, KEY_VALUE_HEADS, HEAD_SIZE)
    layouts = [layout(lengths[m], window) for m in range(MICRO)]
    positions = jnp.concatenate([l[0] for l in layouts])
    cosine_table, sine_table = tables(positions, HEAD_SIZE // 2)
    cosine_table = cosine_table[:, None, :]
    sine_table = sine_table[:, None, :]
    query_hat, query_inv = norm_rows(query_proj, q_gain)
    key_hat, key_inv = norm_rows(key_proj, k_gain)
    query_low = rotate_halves(query_hat, cosine_table, sine_table, 1.0).astype(low)
    key_low = rotate_halves(key_hat, cosine_table, sine_table, 1.0).astype(low)
    group = QUERY_HEADS // KEY_VALUE_HEADS

    def heads(values, per):
        return jnp.moveaxis(values.reshape(MICRO, window, KEY_VALUE_HEADS, per, HEAD_SIZE), 2, 1)

    q_heads = heads(query_low, group)
    k_heads = heads(key_low, 1)[:, :, :, 0]
    v_heads = heads(value_low, 1)[:, :, :, 0]
    mixtures = []
    logs = []
    for m in range(MICRO):
        mixture, log_totals = lax.map(partial(attend_forward, layouts[m][1]), (q_heads[m], k_heads[m], v_heads[m]))
        mixtures.append(jnp.moveaxis(mixture, 0, 1).reshape(window, q_width).astype(low))
        logs.append(log_totals)
    attended = jnp.concatenate(mixtures, axis=0)
    resid = inputs + jnp.dot(attended, out_all, preferred_element_type=f32)
    normed_two, inverse_two = norm_rows(resid, ffn_gain_all)
    ffn_low = normed_two.astype(low)

    gate_proj, up_proj, hidden_t = ffn_forward(ffn_low, gate_up_all)
    hid_blocks = hidden_t.reshape(-1, 2, 2, 2, w_down.shape[0], rows)

    down_parts = []
    bit_c = place & 1
    bit_x = (place >> 1) & 1
    for flip_c in (0, 1):
        for flip_x in (0, 1):
            part = lax.dynamic_index_in_dim(hid_blocks, bit_c ^ flip_c, 3, False)
            part = lax.dynamic_index_in_dim(part, bit_x ^ flip_x, 2, False)
            down_parts.append(part.reshape(-1, rows))
    dot_down = lambda left: jnp.dot(left, window_grads, preferred_element_type=f32)
    quarter = down_parts[0].shape[0]
    first = jnp.concatenate([dot_down(down_parts[2]).astype(low), dot_down(down_parts[3]).astype(low)], axis=0)
    got = hop(first, 0, count)
    second = (dot_down(down_parts[1]) + got[quarter:].astype(f32)).astype(low)
    received = hop(second, 1, count)
    kept = (dot_down(down_parts[0]) + got[:quarter].astype(f32)).astype(low)
    for bit in range(2, levels):
        shape = (-1, 2, w_down.shape[0], width)
        mine = (place >> bit) & 1
        kept = kept.reshape(shape)
        received = received.reshape(shape)
        both = lambda at: (
            lax.dynamic_index_in_dim(kept, at, 1, False).astype(f32)
            + lax.dynamic_index_in_dim(received, at, 1, False).astype(f32)
        ).astype(low)
        sent = both(1 - mine)
        kept = both(mine)
        received = hop(sent, bit, count)
    grad_down = (kept.astype(f32) + received.astype(f32)).reshape(w_down.shape)

    grad_gate_low, grad_up_low, output, grad_normed_two = ffn_backward(
        gate_proj, up_proj, window_grads, resid, gate_up_all, down_all
    )
    output_rows = from_windows(output)

    select_plain = owner_select(place, plain, count, width)
    select_turned = owner_select(place, turned, count, width)
    grad_gate = product_scatter(quarters(select_rows(select_turned, ffn_low)), grad_gate_low, turned, count)
    ffn_plain = quarters(select_rows(select_plain, ffn_low))
    grad_up = product_scatter(ffn_plain, grad_up_low, plain, count)

    grad_resid_part, ffn_rows = norm_back(grad_normed_two, resid, inverse_two, ffn_gain_all)
    grad_resid = window_grads.astype(f32) + grad_resid_part
    branch_low = grad_resid.astype(low)
    att_gradient = ntdot(branch_low, out_all).astype(low)
    grad_out = product_scatter(quarters(select_rows(select_turned, attended)), branch_low, turned, count)
    head_gradient = heads(att_gradient, group)
    back_parts = [
        lax.map(
            partial(attend_backward, layouts[m][1]),
            (q_heads[m], k_heads[m], v_heads[m], head_gradient[m], logs[m]),
        )
        for m in range(MICRO)
    ]

    def join(at, per):
        return jnp.concatenate([jnp.moveaxis(b[at], 0, 1).reshape(window, per, HEAD_SIZE) for b in back_parts], axis=0)

    dq_rot = join(0, QUERY_HEADS)
    dk_rot = join(1, KEY_VALUE_HEADS)
    dv_low = join(2, KEY_VALUE_HEADS).reshape(rows, k_width).astype(low)
    dq_hat = rotate_halves(dq_rot, cosine_table, sine_table, -1.0)
    dk_hat = rotate_halves(dk_rot, cosine_table, sine_table, -1.0)
    dq_proj, query_rows = norm_back(dq_hat, query_proj, query_inv, q_gain)
    dk_proj, key_rows = norm_back(dk_hat, key_proj, key_inv, k_gain)
    dqkv = jnp.concatenate(
        [dq_proj.reshape(rows, q_width).astype(low), dk_proj.reshape(rows, k_width).astype(low), dv_low], axis=1
    )
    grad_qkv = product_scatter(quarters(select_rows(select_plain, normed_low)), dqkv, plain, count)
    grad_normed = ntdot(dqkv, qkv_all)
    grad_input_part, attn_rows = norm_back(grad_normed, inputs, inverse_one, attn_gain_all)
    input_grad = (grad_resid + grad_input_part).astype(low)
    grad_rows = from_windows(input_grad)

    small = jnp.concatenate(
        [
            jnp.sum(attn_rows, axis=0),
            jnp.sum(ffn_rows, axis=0),
            jnp.sum(query_rows, axis=(0, 1)),
            jnp.sum(key_rows, axis=(0, 1)),
        ]
    ).reshape(-1, 128)
    for bit in range(levels):
        small = small + hop(small, bit, count)
    small = small.reshape(-1)
    own = lambda start: lax.dynamic_slice(small, (start + place * share_width,), (share_width,))
    return (
        output_rows,
        grad_rows,
        own(0),
        grad_qkv[:, :q_width],
        grad_qkv[:, q_width : q_width + k_width],
        grad_qkv[:, q_width + k_width :],
        small[2 * width : 2 * width + HEAD_SIZE],
        small[2 * width + HEAD_SIZE :],
        grad_out,
        own(width),
        grad_gate,
        grad_up,
        grad_down,
    )


def solution(mesh):
    in_specs = (
        P("dp", None),
        P("dp", None),
        P("dp", None),
        P("dp", None),
        P("dp"),
        P("dp", None),
        P("dp", None),
        P("dp", None),
        P(),
        P(),
        P("dp", None),
        P("dp"),
        P("dp", None),
        P("dp", None),
        P("dp", None),
    )
    out_specs = (
        P("dp", None),
        P("dp", None),
        P("dp"),
        P("dp", None),
        P("dp", None),
        P("dp", None),
        P(),
        P(),
        P("dp", None),
        P("dp"),
        P("dp", None),
        P("dp", None),
        P("dp", None),
    )
    return jax.shard_map(
        per_device, mesh=mesh, in_specs=in_specs, out_specs=out_specs, check_vma=False
    )
```

```python
import jax
import jax.numpy as jnp
from jax import lax
from jax.experimental import pallas as pl
from jax.experimental.pallas import tpu as pltpu
from jax.sharding import PartitionSpec as P

QUERY_HEADS = 16
KEY_VALUE_HEADS = 8
HEAD_SIZE = 64
WINDOW_TOKENS = 256
MICRO = 2


EPS = 1e-05
THETA = 1000000.0
NEGATIVE = -1e30


def tdot(left, right):
    return lax.dot_general(
        left, right, (((0,), (0,)), ((), ())), preferred_element_type=jnp.float32
    )


def ntdot(left, right):
    return lax.dot_general(
        left, right, (((1,), (1,)), ((), ())), preferred_element_type=jnp.float32
    )


def norm_rows(values, gain):
    inverse = lax.rsqrt(jnp.mean(values * values, axis=-1, keepdims=True) + EPS)
    return (values * inverse * gain, inverse)


def norm_back(grad, values, inverse, gain):
    scaled = grad * gain
    grad_values = inverse * scaled - values * inverse * inverse * inverse * jnp.mean(
        scaled * values, axis=-1, keepdims=True
    )
    return (grad_values, grad * values * inverse)


def tables(positions, half_dim):
    steps_index = jnp.arange(half_dim, dtype=jnp.float32)
    inverse_freq = THETA ** (-steps_index / half_dim)
    angles = positions.astype(jnp.float32)[:, None] * inverse_freq[None, :]
    return (jnp.cos(angles), jnp.sin(angles))


def layout(lengths_row, feature_width):
    places = jnp.arange(feature_width, dtype=jnp.int32)
    ends = jnp.cumsum(lengths_row)
    segment = jnp.sum((places[:, None] >= ends[None, :]).astype(jnp.int32), axis=1)
    starts = ends - lengths_row
    picked = segment[:, None] == jnp.arange(lengths_row.shape[0], dtype=jnp.int32)[None, :]
    begins = jnp.sum(jnp.where(picked, starts[None, :], 0), axis=1)
    allowed = (segment[:, None] == segment[None, :]) & (places[None, :] <= places[:, None])
    return (places - begins, allowed)


CHUNKS = 32
FLOOR = pl.CostEstimate(flops=0, bytes_accessed=1 << 16, transcendentals=0)
ANYWHERE = pl.BlockSpec(memory_space=pltpu.HBM)
F32 = jnp.float32
LOW = jnp.bfloat16


def label(body):
    parts = [p for p in body.__qualname__.split('.') if not p.startswith('<') and p != 'body']
    return '_'.join(parts).lower()


def run(body, operands, in_specs, out_shape, out_specs, grid=(1,), scratch=(), deps=(), vmem=60, aliases=None, carry=()):
    deps = tuple(deps)
    carry = tuple(carry)
    inputs = len(operands)
    skipped = inputs + len(deps) + len(carry)
    single = not isinstance(out_shape, (list, tuple))
    out_shape = [out_shape] if single else list(out_shape)
    out_specs = [out_specs] if single else list(out_specs)
    outputs = len(out_shape)

    def wrapped(*refs):
        body(*refs[:inputs], *refs[skipped : skipped + outputs], *refs[skipped + outputs + len(carry) :])

    aliases = dict(aliases or {})
    for i in range(len(carry)):
        aliases[inputs + len(deps) + i] = outputs + i
    outs = pl.pallas_call(
        wrapped,
        grid=grid,
        in_specs=list(in_specs) + [ANYWHERE] * (len(deps) + len(carry)),
        out_specs=out_specs + [ANYWHERE] * len(carry),
        out_shape=out_shape + [jax.ShapeDtypeStruct(c.shape, c.dtype) for c in carry],
        scratch_shapes=list(scratch),
        input_output_aliases=aliases,
        compiler_params=pltpu.CompilerParams(vmem_limit_bytes=vmem << 20),
        cost_estimate=FLOOR,
        name=label(body),
    )(*operands, *deps, *carry)
    own = outs[0] if single else outs[:outputs]
    return (own, list(outs[outputs:])) if carry else own


def hop(values, bit, count):
    return lax.ppermute(values, "dp", [(i, i ^ (1 << bit)) for i in range(count)])


def position_masks(order, count):
    bits = len(order)
    position = jnp.arange(count, dtype=jnp.int32)
    mask = jnp.zeros_like(position)
    for at, bit in enumerate(order):
        mask = mask | (((position >> (bits - 1 - at)) & 1) << bit)
    return mask


def owner_select(place, order, count, width):
    share = width // count
    column = jnp.arange(width, dtype=jnp.int32)
    feature = (place ^ jnp.repeat(position_masks(order, count), share)) * share + column % share
    return (jnp.arange(width, dtype=jnp.int32)[:, None] == feature[None, :]).astype(LOW)


def select_rows(selects, values, deps=()):
    rows, width = values[0].shape

    def body(*refs):
        count = len(values)
        for i in range(count):
            refs[2 * count][i] = lax.dot_general(
                refs[i][...], refs[count + i][...], (((0,), (1,)), ((), ())), preferred_element_type=F32
            ).astype(LOW)

    whole = lambda a: pl.BlockSpec(a.shape, lambda i: (0, 0))
    operands = [*selects, *values]
    return run(
        body,
        operands,
        [whole(a) for a in operands],
        jax.ShapeDtypeStruct((len(values), width, rows), LOW),
        pl.BlockSpec((len(values), width, rows), lambda i: (0, 0, 0)),
        deps=deps,
    )


def order_blocks(blocks, place, order):
    count, share, tokens = blocks.shape
    rest = order[1:-2]

    def mask_of(t):
        mask = 0
        for at, bit in enumerate(rest):
            mask = mask | (((t >> (len(rest) - 1 - at)) & 1) << bit)
        return mask

    def body(place_ref, blocks_ref, out_ref):
        low = place_ref[0] & 7
        for first in range(2):
            for second in range(2):
                for third in range(2):
                    mask = first | (second << order[-2]) | (third << order[-1])
                    out_ref[first, 0, 2 * second + third] = blocks_ref[low ^ mask]

    ordered = pl.pallas_call(
        body,
        grid_spec=pltpu.PrefetchScalarGridSpec(
            num_scalar_prefetch=1,
            grid=(count // 8,),
            in_specs=[
                pl.BlockSpec((8, share, tokens), lambda t, place_ref: ((place_ref[0] ^ mask_of(t)) >> 3, 0, 0))
            ],
            out_specs=pl.BlockSpec((2, 1, 4, share, tokens), lambda t, place_ref: (0, t, 0, 0, 0)),
        ),
        out_shape=jax.ShapeDtypeStruct((2, count // 8, 4, share, tokens), blocks.dtype),
        compiler_params=pltpu.CompilerParams(vmem_limit_bytes=60 << 20),
        cost_estimate=FLOOR,
        name="order_blocks",
    )(place[None], blocks)
    return ordered.reshape(1, count * share, tokens)


def join(pairs, deps=()):
    operands = []
    shapes = []
    finals = []
    cuts = []
    scratch = []
    for own, received, bit, at in pairs:
        lead = own.shape[:-2]
        rows, columns = own.shape[-2:]
        outer = 1
        for size in lead[:at]:
            outer *= size
        inner = 1
        for size in lead[at:]:
            inner *= size
        operands += [bit[None], own.reshape(outer, inner, rows, columns), received.reshape(outer, inner, rows, columns)]
        shapes.append(jax.ShapeDtypeStruct((outer, 2, inner, rows, columns), own.dtype))
        finals.append(lead[:at] + (2,) + lead[at:] + (rows, columns))
        scratch.append(pltpu.VMEM((2, outer, inner, rows, columns), own.dtype))
        if outer > 1:
            step = max(1, outer // 4)
            cuts.append([(pl.ds(i, step), slice(None)) for i in range(0, outer, step)])
        else:
            step = max(1, inner // 4)
            cuts.append([(slice(None), pl.ds(i, step)) for i in range(0, inner, step)])
    total = 2 * sum(len(c) for c in cuts)

    def body(*refs):
        number = len(pairs)
        outs = refs[3 * number : 4 * number]
        held = refs[4 * number : 5 * number]
        in_sems, out_sems = refs[5 * number :]
        ins = []
        writes = []
        for p in range(number):
            mine = refs[3 * p][0]
            for o, n in cuts[p]:
                for s, target in enumerate((mine, 1 - mine)):
                    k = len(ins)
                    ins.append(pltpu.make_async_copy(refs[3 * p + 1 + s].at[o, n], held[p].at[s, o, n], in_sems.at[k]))
                    writes.append(pltpu.make_async_copy(held[p].at[s, o, n], outs[p].at[o, target, n], out_sems.at[k]))
        for copy in ins:
            copy.start()
        for copy, write in zip(ins, writes):
            copy.wait()
            write.start()
        for write in writes:
            write.wait()

    smem = pl.BlockSpec(memory_space=pltpu.SMEM)
    joined = run(
        body,
        operands,
        [smem, ANYWHERE, ANYWHERE] * len(pairs),
        shapes,
        [ANYWHERE] * len(pairs),
        scratch=scratch + [pltpu.SemaphoreType.DMA((total,)), pltpu.SemaphoreType.DMA((total,))],
        deps=deps,
    )
    return [j.reshape(f) for j, f in zip(joined, finals)]


class Gather:
    def __init__(self, values, orders, place, count):
        self.values = list(values)
        self.orders = orders
        self.have = [[], []]
        self.place = place
        self.count = count
        self.step = 0
        self.send()

    def send(self):
        if self.step < len(self.orders[0]):
            self.received = [hop(v, o[self.step], self.count) for v, o in zip(self.values, self.orders)]

    def take(self, deps=()):
        pairs = []
        for i in range(2):
            bit = self.orders[i][self.step]
            at = sum(1 for other in self.have[i] if other > bit)
            pairs.append((self.values[i], self.received[i], (self.place >> bit) & 1, at))
            self.have[i].append(bit)
        self.values = join(pairs, deps)
        self.step += 1
        self.send()
        return self.values[0]

    def result(self):
        return [v.reshape(-1, v.shape[-1]) for v in self.values]


class Slot:
    def __init__(self, count):
        self.count = count
        self.pending = []

    def run(self, take, sends, *args, **kwargs):
        carried = [array for _, _, arrays in self.pending for array in arrays]
        kept = [d for d in kwargs.pop("deps", ()) if not any(d is c for c in carried)]
        outs = run(*args, carry=carried, deps=kept, **kwargs)
        if carried:
            outs, carried = outs
            fresh = []
            for owner, bits, arrays in self.pending:
                fresh.append((owner, bits, carried[: len(arrays)]))
                carried = carried[len(arrays) :]
            self.pending = fresh
        self.pending.append(take(outs))
        return sends(outs)

    def hold(self, array):
        self.pending.append((None, (), [array]))

    def start(self):
        held = []
        for owner, bits, arrays in self.pending:
            if owner is None:
                held += arrays
            else:
                owner.received = [hop(a, b, self.count) for a, b in zip(arrays, bits)]
        self.pending = []
        return held


class Scatter:
    def __init__(self, lefts, pick, rights, tile, orders):
        self.lefts, self.pick, self.rights, self.tile = lefts, pick, rights, tile
        self.orders = orders
        self.half = lefts.shape[1] // 2
        self.tokens = lefts.shape[2]
        self.step = 0
        self.starts = [sum(r[2] for r in rights[:i]) for i in range(len(rights))]
        self.tiles = sum(r[2] for r in rights)

    def within(self, part):
        start, tiles = self.starts[part], self.rights[part][2]
        return lambda t: jnp.clip(t - start, 0, tiles - 1)

    def specs(self, rows_at):
        tile, tokens, pick = self.tile, self.tokens, self.pick
        specs = [pl.BlockSpec((1, self.half, tokens), lambda t: (pick(t), rows_at, 0))]
        for part, (_, first, _) in enumerate(self.rights):
            at = self.within(part)
            specs.append(pl.BlockSpec((tokens, tile), lambda t, at=at, first=first: (0, first + at(t))))
        return specs

    def each(self, act):
        t = pl.program_id(0)
        for part, (_, _, tiles) in enumerate(self.rights):
            start = self.starts[part]
            pl.when((t >= start) & (t < start + tiles))(lambda part=part: act(part))

    def bits(self, number):
        return [order[self.step] for order in self.orders[:number]]

    def first(self, slot, deps=()):
        number = len(self.rights)

        def body(left_ref, *refs):
            def act(part):
                refs[number][...] = jnp.dot(left_ref[0], refs[part][...], preferred_element_type=F32).astype(LOW)

            self.each(act)

        bits = self.bits(1)
        self.step = 1
        return slot.run(
            lambda sent: (self, bits, [sent]),
            lambda sent: sent,
            body,
            [self.lefts, *[r[0] for r in self.rights]],
            self.specs(1),
            jax.ShapeDtypeStruct((self.half, self.tiles * self.tile), LOW),
            pl.BlockSpec((self.half, self.tile), lambda t: (0, t)),
            grid=(self.tiles,),
            deps=deps,
        )

    def keep(self, outs):
        self.kept = [outs[i] for i in range(1, len(outs), 2)]
        return self.kept[0]

    def second(self, slot, deps=()):
        tile, quarter, number = self.tile, self.half // 2, len(self.rights)

        def body(left_ref, *refs):
            got_ref = refs[number]
            outs = refs[number + 1 :]

            def act(part):
                total = jnp.dot(left_ref[0], refs[part][...], preferred_element_type=F32) + got_ref[...].astype(F32)
                total = total.astype(LOW)
                outs[2 * part][...] = total[quarter:]
                outs[2 * part + 1][...] = total[:quarter]

            self.each(act)

        shapes = []
        specs = []
        for part, (_, _, tiles) in enumerate(self.rights):
            at = self.within(part)
            shapes += [jax.ShapeDtypeStruct((quarter, tiles * tile), LOW)] * 2
            specs += [pl.BlockSpec((quarter, tile), lambda t, at=at: (0, at(t)))] * 2
        bits = self.bits(number)
        self.step = 2
        return slot.run(
            lambda outs: (self, bits, [outs[i] for i in range(0, len(outs), 2)]),
            self.keep,
            body,
            [self.lefts, *[r[0] for r in self.rights], self.received[0]],
            self.specs(0) + [pl.BlockSpec((self.half, tile), lambda t: (0, t))],
            shapes,
            specs,
            grid=(self.tiles,),
            deps=deps,
        )

    def add(self, slot, deps=()):
        number = len(self.kept)
        joined = len(self.kept[0].shape) == 3
        joining = not joined and self.step >= 3
        rows, columns = self.kept[0].shape[-2:]
        parts = self.kept[0].shape[0] if joined else number
        half = rows // 2
        cut = columns
        while cut % 256 == 0 and parts * rows * cut > 700 * 1024:
            cut //= 2

        def body(*refs):
            ins, outs = refs[: 2 * number], refs[2 * number :]
            for p in range(number):
                total = (ins[2 * p][...].astype(F32) + ins[2 * p + 1][...].astype(F32)).astype(LOW)
                if joined:
                    outs[0][...] = total[:, half:]
                    outs[1][...] = total[:, :half]
                elif joining:
                    outs[0][p] = total[half:]
                    outs[1][p] = total[:half]
                else:
                    outs[2 * p][...] = total[half:]
                    outs[2 * p + 1][...] = total[:half]

        operands = [a for pair in zip(self.kept, self.received) for a in pair]
        flat = lambda size: pl.BlockSpec((size, cut), lambda t: (0, t))
        deep = lambda size: pl.BlockSpec((parts, size, cut), lambda t: (0, 0, t))
        if joined or joining:
            shapes = [jax.ShapeDtypeStruct((parts, half, columns), LOW)] * 2
            specs = [deep(half)] * 2
        else:
            shapes = [jax.ShapeDtypeStruct((half, columns), LOW)] * (2 * number)
            specs = [flat(half)] * (2 * number)
        bits = self.bits(1 if joined or joining else number)
        self.step += 1
        return slot.run(
            lambda outs: (self, bits, [outs[i] for i in range(0, len(outs), 2)]),
            self.keep,
            body,
            operands,
            [deep(rows) if joined else flat(rows)] * len(operands),
            shapes,
            specs,
            grid=(columns // cut,),
            deps=deps,
        )


class Merged(Scatter):
    def __init__(self, slot, scatters, units, deps=()):
        first = scatters[0]
        self.orders = first.orders
        self.step = first.step
        number = len(first.kept)
        halves = [scatter.kept[0].shape[0] // 2 for scatter in scatters]
        columns = [scatter.kept[0].shape[1] for scatter in scatters]
        operands = []
        for scatter in scatters:
            for kept, received in zip(scatter.kept, scatter.received):
                operands += [kept, received]
        if units is None:
            shape = (number, halves[0], sum(columns))
        else:
            owners = halves[0] // units[0]
            shape = (number, owners * sum(units), columns[0])

        def body(*refs):
            ins, outs = refs[: len(operands)], refs[len(operands) :]
            for i in range(len(scatters)):
                half = halves[i]
                for p in range(number):
                    at = 2 * (i * number + p)
                    total = (ins[at][...].astype(F32) + ins[at + 1][...].astype(F32)).astype(LOW)
                    for out_ref, begin in zip(outs, (half, 0)):
                        if units is None:
                            left = sum(columns[:i])
                            out_ref[p, :, left : left + columns[i]] = total[begin : begin + half]
                            continue
                        for owner in range(owners):
                            top = owner * sum(units) + sum(units[:i])
                            source = begin + owner * units[i]
                            out_ref[p, top : top + units[i], :] = total[source : source + units[i]]

        bits = self.bits(1)
        self.step += 1
        out = jax.ShapeDtypeStruct(shape, LOW)
        slot.run(
            lambda outs: (self, bits, [outs[0]]),
            self.keep,
            body,
            operands,
            [pl.BlockSpec(a.shape, lambda t: (0, 0)) for a in operands],
            [out, out],
            [pl.BlockSpec(shape, lambda t: (0, 0, 0))] * 2,
            deps=deps,
        )


def finish(scatters, places, shapes, deps=()):
    operands = []
    for scatter in scatters:
        operands += [scatter.kept[0], scatter.received[0]]

    def body(*refs):
        ins, outs = refs[: len(operands)], refs[len(operands) :]
        totals = {}
        for which, part, from_rows, from_columns, out, rows, columns in places:
            if (which, part) not in totals:
                totals[which, part] = ins[2 * which][part].astype(F32) + ins[2 * which + 1][part].astype(F32)
            outs[out][rows, columns] = totals[which, part][from_rows, from_columns]

    return run(
        body,
        operands,
        [pl.BlockSpec(a.shape, lambda t: (0, 0, 0)) for a in operands],
        [jax.ShapeDtypeStruct(shape, F32) for shape in shapes],
        [pl.BlockSpec(shape, lambda t: (0, 0)) for shape in shapes],
        deps=deps,
    )


def head_sum(values, ones):
    high = values.astype(jnp.bfloat16)
    rest = (values - high.astype(jnp.float32)).astype(jnp.bfloat16)
    return jnp.dot(high, ones, preferred_element_type=jnp.float32) + jnp.dot(
        rest, ones, preferred_element_type=jnp.float32
    )


def swap_halves(values):
    lane = lax.broadcasted_iota(jnp.int32, values.shape, 1)
    return jnp.where(
        lane % HEAD_SIZE < HEAD_SIZE // 2,
        pltpu.roll(values, 2 * HEAD_SIZE - HEAD_SIZE // 2, 1),
        pltpu.roll(values, HEAD_SIZE // 2, 1),
    )


def lower_lanes(values):
    return lax.broadcasted_iota(jnp.int32, values.shape, 1) < HEAD_SIZE


def head_ones():
    row = lax.broadcasted_iota(jnp.int32, (2 * HEAD_SIZE, 2 * HEAD_SIZE), 0) // HEAD_SIZE
    column = lax.broadcasted_iota(jnp.int32, (2 * HEAD_SIZE, 2 * HEAD_SIZE), 1) // HEAD_SIZE
    return (row == column).astype(jnp.bfloat16)


def spread(pair, which):
    other = pltpu.roll(pair.astype(jnp.float32), HEAD_SIZE, 1)
    pair = pair.astype(jnp.float32)
    left, right = (pair, other) if which == 0 else (other, pair)
    low = lower_lanes(pair)
    zero = jnp.zeros_like(pair)
    return jnp.concatenate([jnp.where(low, left, zero), jnp.where(low, zero, right)], axis=0).astype(jnp.bfloat16)


def spread_ones(rows):
    row = lax.broadcasted_iota(jnp.int32, (2 * rows, 2 * HEAD_SIZE), 0) // rows
    column = lax.broadcasted_iota(jnp.int32, (2 * rows, 2 * HEAD_SIZE), 1) // HEAD_SIZE
    return (row == column).astype(jnp.bfloat16)


def attend_kernel(q_ref, k_ref, v_ref, cos_ref, sin_ref, qg_ref, kg_ref, bias_ref, qs_ref, kl_ref, vl_ref, att_ref):
    ones = head_ones()
    cosine = cos_ref[...]
    sine = sin_ref[...]
    bias = bias_ref[0]
    bias = jnp.concatenate([bias, bias], axis=1)
    rows = cosine.shape[0]
    tail = spread_ones(rows)

    def turn(values, gain):
        inverse = lax.rsqrt(head_sum(values * values, ones) * (1.0 / HEAD_SIZE) + EPS)
        normed = values * inverse * gain
        return normed * cosine + swap_halves(normed) * sine

    keys = turn(k_ref[...], kg_ref[...]).astype(jnp.bfloat16)
    kl_ref[...] = keys
    values = v_ref[...].astype(jnp.bfloat16)
    vl_ref[...] = values
    for which in range(2):
        lanes = slice(which * 2 * HEAD_SIZE, (which + 1) * 2 * HEAD_SIZE)
        queries = turn(q_ref[:, lanes], qg_ref[...]).astype(jnp.bfloat16) * (HEAD_SIZE**-0.5)
        queries = queries.astype(jnp.bfloat16)
        qs_ref[:, lanes] = queries
        scores = ntdot(queries, spread(keys, which)) + bias
        exponent = jnp.exp(scores).astype(jnp.bfloat16)
        both = jnp.concatenate([spread(values, which), tail], axis=1)
        mixed = jnp.dot(exponent, both, preferred_element_type=jnp.float32)
        att_ref[:, lanes] = (mixed[:, : 2 * HEAD_SIZE] / mixed[:, 2 * HEAD_SIZE :]).astype(jnp.bfloat16)


def attend(proj, cosine, sine, query_gain, key_gain, bias, deps=()):
    window = bias.shape[1]
    rows = proj.shape[0]
    pair = 2 * HEAD_SIZE
    pairs = KEY_VALUE_HEADS // 2
    k_at = QUERY_HEADS * HEAD_SIZE // pair
    gain = pl.BlockSpec((1, pair), lambda m, p: (0, 0))
    table = pl.BlockSpec((window, pair), lambda m, p: (m, 0))
    wide = pl.BlockSpec((window, 2 * pair), lambda m, p: (m, p))
    thin = pl.BlockSpec((window, pair), lambda m, p: (m, p))
    return run(
        attend_kernel,
        [proj, proj, proj, cosine, sine, query_gain, key_gain, bias],
        [
            wide,
            pl.BlockSpec((window, pair), lambda m, p: (m, k_at + p)),
            pl.BlockSpec((window, pair), lambda m, p: (m, k_at + pairs + p)),
            table,
            table,
            gain,
            gain,
            pl.BlockSpec((1, window, window), lambda m, p: (m, 0, 0)),
        ],
        [
            jax.ShapeDtypeStruct((rows, QUERY_HEADS * HEAD_SIZE), LOW),
            jax.ShapeDtypeStruct((rows, KEY_VALUE_HEADS * HEAD_SIZE), LOW),
            jax.ShapeDtypeStruct((rows, KEY_VALUE_HEADS * HEAD_SIZE), LOW),
            jax.ShapeDtypeStruct((rows, QUERY_HEADS * HEAD_SIZE), LOW),
        ],
        [wide, thin, thin, wide],
        grid=(MICRO, pairs),
        deps=deps,
    )


def attend_back_kernel(
    q_ref, k_ref, qs_ref, kl_ref, vl_ref, att_ref, da_ref, cos_ref, sin_ref, qg_ref, kg_ref, bias_ref,
    room_ref, grad_ref, ov_ref, gains_ref,
):
    pair = pl.program_id(1)
    ones = head_ones()
    cosine = cos_ref[...]
    sine = sin_ref[...]
    bias = bias_ref[0]
    bias = jnp.concatenate([bias, bias], axis=1)
    rows = cosine.shape[0]
    tail = spread_ones(rows)
    low = jnp.bfloat16

    def unturn(grad, values, gain):
        inverse = lax.rsqrt(head_sum(values * values, ones) * (1.0 / HEAD_SIZE) + EPS)
        back = grad * cosine - swap_halves(grad) * sine
        scaled = back * gain
        mean = head_sum(scaled * values, ones) * (1.0 / HEAD_SIZE)
        grad_values = inverse * scaled - values * (inverse * inverse * inverse) * mean
        return (grad_values.astype(low), jnp.sum(back * values * inverse, axis=0, keepdims=True))

    keys = kl_ref[...]
    values = vl_ref[...]
    query_sum = jnp.zeros((1, 2 * HEAD_SIZE), jnp.float32)
    key_grads = []
    value_grads = []
    for which in range(2):
        lanes = slice(which * 2 * HEAD_SIZE, (which + 1) * 2 * HEAD_SIZE)
        queries = qs_ref[:, lanes]
        grads = da_ref[:, lanes]
        wide_keys = spread(keys, which)
        exponent = jnp.exp(ntdot(queries, wide_keys) + bias)
        exponent_low = exponent.astype(low)
        inverse = 1.0 / jnp.dot(exponent_low, tail, preferred_element_type=jnp.float32)
        grads_wide = grads.astype(jnp.float32)
        inner = (-grads_wide * att_ref[:, lanes].astype(jnp.float32)).astype(low)
        shifted = ntdot(
            jnp.concatenate([grads, inner], axis=1), jnp.concatenate([spread(values, which), tail], axis=1)
        )
        score_grads = (exponent * shifted).astype(low)
        query_grad = jnp.dot(score_grads, wide_keys, preferred_element_type=jnp.float32) * (
            inverse * (HEAD_SIZE**-0.5)
        )
        grad_low, gain_rows = unturn(query_grad, q_ref[:, lanes], qg_ref[...])
        at = pl.multiple_of(pair * (4 * HEAD_SIZE) + which * 2 * HEAD_SIZE, 2 * HEAD_SIZE)
        grad_ref[:, pl.ds(at, 2 * HEAD_SIZE)] = grad_low
        query_sum = query_sum + gain_rows
        key_grads.append(tdot(score_grads, (queries.astype(jnp.float32) * inverse).astype(low)))
        value_grads.append(tdot(exponent_low, (grads_wide * inverse).astype(low)))

    def fold(parts):
        first = parts[0][:rows] + pltpu.roll(parts[0][rows:], HEAD_SIZE, 1)
        second = pltpu.roll(parts[1][:rows], HEAD_SIZE, 1) + parts[1][rows:]
        return jnp.where(lower_lanes(first), first, second)

    at = pl.multiple_of(pair * (2 * HEAD_SIZE), 2 * HEAD_SIZE)
    ov_ref[:, pl.ds(at, 2 * HEAD_SIZE)] = fold(value_grads).astype(low)
    grad_low, key_sum = unturn(fold(key_grads), k_ref[...], kg_ref[...])
    at = pl.multiple_of(QUERY_HEADS * HEAD_SIZE + pair * (2 * HEAD_SIZE), 2 * HEAD_SIZE)
    grad_ref[:, pl.ds(at, 2 * HEAD_SIZE)] = grad_low

    @pl.when((pl.program_id(0) == 0) & (pair == 0))
    def _():
        gains_ref[...] = jnp.zeros_like(gains_ref)

    gains_ref[0:1, :] += query_sum
    gains_ref[1:2, :] += key_sum


def attend_back(proj, saved, att_grads, grad_ov, cosine, sine, query_gain, key_gain, bias, deps=()):
    window = bias.shape[1]
    rows = proj.shape[0]
    pair = 2 * HEAD_SIZE
    pairs = KEY_VALUE_HEADS // 2
    q_width = QUERY_HEADS * HEAD_SIZE
    k_width = KEY_VALUE_HEADS * HEAD_SIZE
    k_at = q_width // pair
    gain = pl.BlockSpec((1, pair), lambda m, p: (0, 0))
    table = pl.BlockSpec((window, pair), lambda m, p: (m, 0))
    wide = pl.BlockSpec((window, 2 * pair), lambda m, p: (m, p))
    thin = pl.BlockSpec((window, pair), lambda m, p: (m, p))
    queries, keys, values, attended = saved
    return run(
        attend_back_kernel,
        [proj, proj, queries, keys, values, attended, att_grads, cosine, sine, query_gain, key_gain, bias, grad_ov],
        [
            wide,
            pl.BlockSpec((window, pair), lambda m, p: (m, k_at + p)),
            wide,
            thin,
            thin,
            wide,
            wide,
            table,
            table,
            gain,
            gain,
            pl.BlockSpec((1, window, window), lambda m, p: (m, 0, 0)),
            ANYWHERE,
        ],
        [
            jax.ShapeDtypeStruct((rows, q_width + k_width), LOW),
            jax.ShapeDtypeStruct(grad_ov.shape, LOW),
            jax.ShapeDtypeStruct((8, pair), jnp.float32),
        ],
        [
            pl.BlockSpec((window, q_width + k_width), lambda m, p: (m, 0)),
            pl.BlockSpec((window, k_width), lambda m, p: (m, q_width // k_width)),
            pl.BlockSpec((8, pair), lambda m, p: (0, 0)),
        ],
        grid=(MICRO, pairs),
        deps=deps,
        aliases={12: 1},
    )


def project(tokens, gain, query_key, value_out, deps=()):
    rows, width = tokens.shape
    qk_width = query_key.shape[1]
    v_width = KEY_VALUE_HEADS * HEAD_SIZE
    tile = WINDOW_TOKENS

    def body(x_ref, gain_ref, qk_ref, v_ref, n1_ref, proj_ref):
        normed, _ = norm_rows(x_ref[...].astype(F32), gain_ref[...])
        normed = normed.astype(LOW)
        n1_ref[...] = normed
        proj_ref[:, :qk_width] = jnp.dot(normed, qk_ref[...], preferred_element_type=F32)
        proj_ref[:, qk_width:] = jnp.dot(normed, v_ref[...], preferred_element_type=F32)

    return run(
        body,
        [tokens, gain, query_key, value_out],
        [
            pl.BlockSpec((tile, width), lambda i: (i, 0)),
            pl.BlockSpec((1, width), lambda i: (0, 0)),
            pl.BlockSpec((width, qk_width), lambda i: (0, 0)),
            pl.BlockSpec((width, v_width), lambda i: (0, width // v_width)),
        ],
        [jax.ShapeDtypeStruct((rows, width), LOW), jax.ShapeDtypeStruct((rows, qk_width + v_width), F32)],
        [
            pl.BlockSpec((tile, width), lambda i: (i, 0)),
            pl.BlockSpec((tile, qk_width + v_width), lambda i: (i, 0)),
        ],
        grid=(rows // tile,),
        deps=deps,
    )


def residual(tokens, attended, value_out, gain, deps=()):
    rows, width = tokens.shape
    tile = WINDOW_TOKENS

    def body(x_ref, att_ref, out_ref, gain_ref, h1_ref, n2_ref):
        h1 = x_ref[...].astype(F32) + jnp.dot(att_ref[...], out_ref[...], preferred_element_type=F32)
        h1_ref[...] = h1
        n2_ref[...] = norm_rows(h1, gain_ref[...])[0].astype(LOW)

    row = pl.BlockSpec((tile, width), lambda i: (i, 0))
    return run(
        body,
        [tokens, attended, value_out, gain],
        [row, row, pl.BlockSpec((width, width), lambda i: (0, 0)), pl.BlockSpec((1, width), lambda i: (0, 0))],
        [jax.ShapeDtypeStruct((rows, width), F32), jax.ShapeDtypeStruct((rows, width), LOW)],
        [row, row],
        grid=(rows // tile,),
        deps=deps,
    )


def ffn_shards(w_gate, w_up, w_down, devices):
    rows, hidden = w_gate.shape
    owned, width = w_down.shape
    unit = hidden // devices
    split = unit * 5 // 9
    bounds = [(0, split), (split, unit)]
    cuts = [(end - begin) * devices for begin, end in bounds]
    down_cuts = [(owned * begin // unit, owned * end // unit) for begin, end in bounds]
    depth = [(end - begin) * width // (2 * cut) for (begin, end), cut in zip(down_cuts, cuts)]

    def body(gate_ref, up_ref, down_ref, first_ref, second_ref):
        for (begin, end), cut, (top, bottom), deep, out_ref in zip(
            bounds, cuts, down_cuts, depth, (first_ref, second_ref)
        ):
            for source_ref, at in ((gate_ref, 0), (up_ref, cut)):
                source = source_ref[...].astype(F32)
                for i in range(devices):
                    size = end - begin
                    out_ref[:rows, at + i * size : at + (i + 1) * size] = source[
                        :, i * unit + begin : i * unit + end
                    ].astype(LOW)
            for q in range((bottom - top) // deep):
                out_ref[rows:, q * width : (q + 1) * width] = down_ref[top + q * deep : top + (q + 1) * deep, :]

    whole = lambda a: pl.BlockSpec(a.shape, lambda i: (0, 0))
    shapes = [jax.ShapeDtypeStruct((rows + deep, 2 * cut), LOW) for deep, cut in zip(depth, cuts)]
    return run(
        body, [w_gate, w_up, w_down], [whole(a) for a in (w_gate, w_up, w_down)], shapes, [whole(a) for a in shapes]
    )


def ffn_shards_plain(w_gate, w_up, w_down, devices):
    chunks, rows, hidden = w_gate.shape
    width = w_down.shape[2]
    unit = hidden // devices
    split = unit * 5 // 9
    outs = []
    for begin, end in ((0, split), (split, unit)):
        columns = [
            w.reshape(chunks, rows, devices, unit)[..., begin:end].reshape(chunks, rows, -1) for w in (w_gate, w_up)
        ]
        down = w_down.reshape(chunks, -1, unit, width)[:, :, begin:end].reshape(chunks, -1, width)
        pieces = 2 * columns[0].shape[2] // width
        down = down.reshape(chunks, pieces, -1, width).transpose(0, 2, 1, 3).reshape(chunks, -1, pieces * width)
        outs.append(jnp.concatenate([jnp.concatenate(columns, axis=2), down], axis=1))
    return outs


def gather_ffn(w_gate, w_up, w_down, count):
    gather = lambda values: lax.all_gather(values, "dp", axis=0, tiled=True)
    if count == CHUNKS:
        return [
            gather(shard).reshape(CHUNKS, shard.shape[0], shard.shape[1])
            for shard in ffn_shards(w_gate, w_up, w_down, count)
        ]
    cut = lambda values: gather(values).reshape(CHUNKS, -1, values.shape[1])
    return ffn_shards_plain(cut(w_gate), cut(w_up), cut(w_down), count)


def set_down(down_ref, held):
    chunks, rows, _ = down_ref.shape
    width = held.shape[1]
    pieces = held.shape[0] // (chunks * rows)
    for i in range(chunks):
        for q in range(pieces):
            at = (i * pieces + q) * rows
            held[at : at + rows, :] = down_ref[i, :, q * width : (q + 1) * width]


def ffn(normed, grads, weight, output, grad_normed, count, last, deps=()):
    rows, width = normed.shape
    share = width // CHUNKS
    hidden = weight.shape[2] // 2
    pieces = 2 * hidden // width
    rest = weight.shape[1] - share
    steps = 4
    tile = hidden // steps
    chunks = CHUNKS // steps
    begins = grad_normed is None

    def body(*refs):
        n2_ref, dy_ref, gate_ref, up_ref, down_ref, y_in_ref = refs[:6]
        hid_ref, dg_ref, du_ref, y_ref, dn_ref, total_y, total_n, held = refs[-8:]
        j = pl.program_id(0)

        @pl.when(j == 0)
        def _():
            total_y[...] = y_in_ref[...]
            total_n[...] = jnp.zeros_like(total_n) if begins else refs[6][...]

        set_down(down_ref, held)
        gate_weight = gate_ref[...].reshape(width, tile)
        up_weight = up_ref[...].reshape(width, tile)
        n2 = n2_ref[...]
        gate = jnp.dot(n2, gate_weight, preferred_element_type=F32)
        up = jnp.dot(n2, up_weight, preferred_element_type=F32)
        dhid = ntdot(dy_ref[...], held[...])
        sig = jax.nn.sigmoid(gate)
        silu = gate * sig
        hid = (silu * up).astype(LOW)
        dgate = (dhid * up * (sig + silu * (1.0 - sig))).astype(LOW)
        dup = (dhid * silu).astype(LOW)
        hid_ref[...] = hid.T
        dg_ref[...] = dgate
        du_ref[...] = dup
        total_y[...] += jnp.dot(hid, held[...], preferred_element_type=F32)
        total_n[...] += ntdot(dgate, gate_weight) + ntdot(dup, up_weight)

        @pl.when(j == pl.num_programs(0) - 1)
        def _():
            dn_ref[...] = total_n[...]
            if last:
                for m in range(MICRO):
                    part = total_y[m * WINDOW_TOKENS : (m + 1) * WINDOW_TOKENS].astype(LOW)
                    y_ref[:, m] = part.reshape(count, WINDOW_TOKENS // count, width)
            else:
                y_ref[...] = total_y[...]

    whole = pl.BlockSpec((rows, width), lambda j: (0, 0))
    cut = pl.BlockSpec((rows, tile), lambda j: (0, j))
    shape = jax.ShapeDtypeStruct((rows, hidden), LOW)
    sums = jax.ShapeDtypeStruct((rows, width), F32)
    dealt = (count, MICRO, WINDOW_TOKENS // count, width)
    return run(
        body,
        [normed, grads, weight, weight, weight, output] + ([] if begins else [grad_normed]),
        [
            whole,
            whole,
            pl.BlockSpec((CHUNKS, share, tile), lambda j: (0, 0, j)),
            pl.BlockSpec((CHUNKS, share, tile), lambda j: (0, 0, j + steps)),
            pl.BlockSpec((chunks, rest, pieces * width), lambda j: (j, share // rest, 0)),
            whole,
        ]
        + ([] if begins else [whole]),
        [
            jax.ShapeDtypeStruct((hidden, rows), LOW),
            shape,
            shape,
            jax.ShapeDtypeStruct(dealt, LOW) if last else sums,
            sums,
        ],
        [
            pl.BlockSpec((tile, rows), lambda j: (j, 0)),
            cut,
            cut,
            pl.BlockSpec(dealt, lambda j: (0, 0, 0, 0)) if last else whole,
            whole,
        ],
        grid=(steps,),
        scratch=[
            pltpu.VMEM((rows, width), F32),
            pltpu.VMEM((rows, width), F32),
            pltpu.VMEM((tile, width), LOW),
        ],
        deps=deps,
    )


def residual_back(grad_normed, resid, grads, gain, value_out, deps=()):
    rows, width = resid.shape
    v_width = KEY_VALUE_HEADS * HEAD_SIZE
    tile = WINDOW_TOKENS

    def body(dn_ref, h1_ref, dy_ref, gain_ref, out_ref, dh_ref, da_ref, datt_ref, sum_ref):
        h1 = h1_ref[...]
        _, inverse = norm_rows(h1, gain_ref[...])
        part, gain_rows = norm_back(dn_ref[...], h1, inverse, gain_ref[...])
        dh1 = dy_ref[...].astype(F32) + part
        low = dh1.astype(LOW)
        dh_ref[...] = dh1
        da_ref[...] = low
        datt_ref[...] = ntdot(low, out_ref[...]).astype(LOW)

        @pl.when(pl.program_id(0) == 0)
        def _():
            sum_ref[...] = jnp.zeros_like(sum_ref)

        sum_ref[...] += jnp.sum(gain_rows, axis=0, keepdims=True)

    row = pl.BlockSpec((tile, width), lambda i: (i, 0))
    one = pl.BlockSpec((1, width), lambda i: (0, 0))
    return run(
        body,
        [grad_normed, resid, grads, gain, value_out],
        [row, row, row, one, pl.BlockSpec((width, width), lambda i: (0, 0))],
        [
            jax.ShapeDtypeStruct((rows, width), F32),
            jax.ShapeDtypeStruct((rows, width + v_width), LOW),
            jax.ShapeDtypeStruct((rows, width), LOW),
            jax.ShapeDtypeStruct((1, width), F32),
        ],
        [row, row, row, one],
        grid=(rows // tile,),
        deps=deps,
    )


def input_back(grad_qk, grad_ov, query_key, value_out, tokens, gain, grad_resid, count, deps=()):
    rows, width = tokens.shape
    qk_width = query_key.shape[1]
    v_width = KEY_VALUE_HEADS * HEAD_SIZE
    tile = WINDOW_TOKENS
    share = tile // count

    def body(qk_ref, v_ref, wqk_ref, wv_ref, x_ref, gain_ref, dh_ref, dx_ref, sum_ref):
        grad = ntdot(qk_ref[...], wqk_ref[...]) + ntdot(v_ref[...], wv_ref[...])
        x = x_ref[...].astype(F32)
        _, inverse = norm_rows(x, gain_ref[...])
        part, gain_rows = norm_back(grad, x, inverse, gain_ref[...])
        dx_ref[:, 0] = (dh_ref[...] + part).astype(LOW).reshape(count, share, width)

        @pl.when(pl.program_id(0) == 0)
        def _():
            sum_ref[...] = jnp.zeros_like(sum_ref)

        sum_ref[...] += jnp.sum(gain_rows, axis=0, keepdims=True)

    row = pl.BlockSpec((tile, width), lambda i: (i, 0))
    one = pl.BlockSpec((1, width), lambda i: (0, 0))
    return run(
        body,
        [grad_qk, grad_ov, query_key, value_out, tokens, gain, grad_resid],
        [
            pl.BlockSpec((tile, qk_width), lambda i: (i, 0)),
            pl.BlockSpec((tile, v_width), lambda i: (i, width // v_width)),
            pl.BlockSpec((width, qk_width), lambda i: (0, 0)),
            pl.BlockSpec((width, v_width), lambda i: (0, width // v_width)),
            row,
            one,
            row,
        ],
        [jax.ShapeDtypeStruct((count, MICRO, share, width), LOW), jax.ShapeDtypeStruct((1, width), F32)],
        [pl.BlockSpec((count, 1, share, width), lambda i: (0, i, 0, 0)), one],
        grid=(rows // tile,),
        deps=deps,
    )


def deal_rows(deal, values, deps=()):
    def body(deal_ref, values_ref, out_ref):
        out_ref[...] = jnp.dot(deal_ref[...], values_ref[...], preferred_element_type=F32).astype(LOW)

    whole = lambda a: pl.BlockSpec(a.shape, lambda i: (0, 0))
    return run(
        body,
        [deal, values],
        [whole(deal), whole(values)],
        jax.ShapeDtypeStruct(values.shape, LOW),
        whole(values),
        deps=deps,
    )


def deal_back(deal, values, width, deps=()):
    def body(deal_ref, values_ref, out_ref):
        out_ref[...] = tdot(deal_ref[...], values_ref[...]).astype(LOW)

    whole = lambda a: pl.BlockSpec(a.shape, lambda i: (0, 0))
    part = pl.BlockSpec((values.shape[0], width), lambda i: (0, 0))
    return run(
        body,
        [deal, values],
        [whole(deal), part],
        jax.ShapeDtypeStruct((values.shape[0], width), LOW),
        part,
        deps=deps,
    )


def per_device(
    tokens,
    cotangent,
    route,
    lengths,
    attn_gain,
    w_query,
    key_weight,
    value_weight,
    query_gain,
    key_norm_gain,
    w_out,
    ffn_gain,
    w_gate,
    w_up,
    w_down,
):
    count = lax.axis_size("dp")
    levels = count.bit_length() - 1
    place = lax.axis_index("dp")
    window = WINDOW_TOKENS
    share = window // count
    width = tokens.shape[1]
    share_width = width // count
    q_width = QUERY_HEADS * HEAD_SIZE
    k_width = KEY_VALUE_HEADS * HEAD_SIZE
    rows = MICRO * window
    half = width // 2
    downward = list(range(levels - 1, -1, -1))
    crossed = list(range(levels - 1, 2, -1)) + [1, 2, 0]
    plain = list(range(levels))
    turned = [0, 2, 1] + list(range(3, levels))
    inward = [0] + list(range(3, levels)) + [1, 2]

    gains = jnp.pad(jnp.stack([attn_gain, ffn_gain], axis=1), ((0, 0), (0, 126)))
    ffn_one, ffn_two = gather_ffn(w_gate, w_up, w_down, count)
    attn = Gather(
        [jnp.concatenate([w_query, key_weight], axis=1), jnp.concatenate([w_out, value_weight, gains], axis=1)],
        [downward, crossed],
        place,
        count,
    )

    orders = route[0].reshape(MICRO, count, share).transpose(1, 0, 2).reshape(rows)
    deal = (orders[:, None] == jnp.arange(rows, dtype=jnp.int32)[None, :]).astype(LOW)

    def exchange(values):
        return lax.all_to_all(values, "dp", split_axis=0, concat_axis=0, tiled=True)

    def to_windows(sent):
        got = exchange(sent).reshape(count, MICRO, share, width)
        return got.transpose(1, 0, 2, 3).reshape(rows, width)

    def returned(values):
        return exchange(values.reshape(rows, values.shape[-1]))

    q_gain = jnp.tile(query_gain.astype(F32), 2)[None, :]
    k_gain = jnp.tile(key_norm_gain.astype(F32), 2)[None, :]
    layouts = [layout(lengths[m], window) for m in range(MICRO)]
    cosine_half, sine_half = tables(jnp.concatenate([l[0] for l in layouts]), HEAD_SIZE // 2)
    cosine = jnp.tile(cosine_half, (1, 4))
    sine = jnp.tile(jnp.concatenate([-sine_half, sine_half], axis=1), (1, 2))
    bias = jnp.where(jnp.stack([l[1] for l in layouts]), 0.0, NEGATIVE).astype(F32)
    select_plain = owner_select(place, plain, count, width)
    select_turned = owner_select(place, turned, count, width)

    tables_ready = [cosine, sine, bias, select_plain, select_turned]
    token = deal
    for step in range(levels):
        token = attn.take([token] + (tables_ready if step == 1 else []))
        if step == levels - 3:
            window_tokens = to_windows(deal_rows(deal, tokens, [token]))
    window_grads = to_windows(deal_rows(deal, cotangent, [token]))
    query_key, out_value = attn.result()
    gain_rows = out_value[:, width + k_width :].astype(F32)
    attn_gain_all = gain_rows[:, 0][None, :]
    ffn_gain_all = gain_rows[:, 1][None, :]

    normed_low, proj = project(window_tokens, attn_gain_all, query_key, out_value)
    queries, keys, values, attended = attend(proj, cosine, sine, q_gain, k_gain, bias)
    resid, ffn_low = residual(window_tokens, attended, out_value, ffn_gain_all)
    lefts_ffn = select_rows([select_plain, select_turned], [ffn_low, ffn_low])
    orders_pair = [plain, turned]
    slot = Slot(count)

    def ffn_sums(hidden_t, grad_gate_low, grad_up_low):
        tile = grad_gate_low.shape[1] // 2
        both = Scatter(
            lefts_ffn, lambda t: t // 2, [(grad_gate_low, 0, 2), (grad_up_low, 0, 2)], tile, orders_pair
        )
        lefts = order_blocks(hidden_t.reshape(count, -1, rows), place, inward)
        return both, Scatter(lefts, lambda t: 0, [(window_grads, 0, 2)], half, [inward])

    hid_one, dg_one, du_one, partial_output, dn_one = ffn(
        ffn_low, window_grads, ffn_one, resid, None, count, False, [lefts_ffn]
    )
    sum_one, down_one = ffn_sums(hid_one, dg_one, du_one)
    token = sum_one.first(slot, [])
    token = down_one.first(slot, [token])
    slot.start()
    lefts_attn = select_rows(
        [select_plain, select_turned, select_turned], [normed_low, attended, normed_low], [token]
    )
    token = sum_one.second(slot, [lefts_attn])
    token = down_one.second(slot, [token])
    slot.start()
    hid_two, dg_two, du_two, output, dn_two = ffn(
        ffn_low, window_grads, ffn_two, partial_output, dn_one, count, True, [token]
    )
    sum_two, down_two = ffn_sums(hid_two, dg_two, du_two)
    token = sum_two.first(slot, [dn_two])
    slot.hold(output)
    token = down_two.first(slot, [token])
    token = sum_one.add(slot, [token])
    token = down_one.add(slot, [token])
    (output,) = slot.start()
    returned_output = returned(output)
    grad_resid, grad_ov, grad_att, ffn_sum = residual_back(dn_two, resid, window_grads, ffn_gain_all, out_value, [token])
    grad_qk, grad_ov, head_gains = attend_back(
        proj, (queries, keys, values, attended), grad_att, grad_ov, cosine, sine, q_gain, k_gain, bias
    )
    sum_attn = Scatter(
        lefts_attn,
        lambda t: jnp.where(t < 3, 0, jnp.where(t < 5, 1, 2)),
        [(grad_qk, 0, 3), (grad_ov, 0, 3)],
        half,
        orders_pair,
    )
    token = sum_two.second(slot, [grad_qk])
    token = down_two.second(slot, [token, *sum_one.received, *down_one.received])
    slot.start()
    token = sum_attn.first(slot, [token])
    token = sum_one.add(slot, [token])
    slot.start()
    input_grad, attn_sum = input_back(
        grad_qk, grad_ov, query_key, out_value, window_tokens, attn_gain_all, grad_resid, count, [token]
    )
    small = jnp.concatenate(
        [
            attn_sum.reshape(count, share_width),
            ffn_sum.reshape(count, share_width),
            jnp.broadcast_to((head_gains[:2, :HEAD_SIZE] + head_gains[:2, HEAD_SIZE:]).reshape(1, -1), (count, 2 * HEAD_SIZE)),
        ],
        axis=1,
    )
    small_high = small.astype(LOW)
    small_rest = (small - small_high.astype(F32)).astype(LOW)
    beside = MICRO * share * 128
    small = jnp.concatenate([small_high, small_rest], axis=1)
    small = jnp.pad(small, ((0, 0), (0, beside - small.shape[1]))).reshape(count, MICRO, share, 128)
    input_grad = jnp.concatenate([input_grad, small], axis=3)
    slot.hold(input_grad)
    token = sum_attn.second(slot, [input_grad])
    token = sum_two.add(slot, [token, *sum_one.received])
    token = down_two.add(slot, [token])
    (input_grad,) = slot.start()
    returned_grads = returned(input_grad)
    output_rows = deal_back(deal, returned_output, width, [token])
    token = output_rows
    if sum_one.step < levels:
        token = sum_one.add(slot, [token])
    token = sum_two.add(slot, [token])
    token = sum_attn.add(slot, [token])
    owned = w_down.shape[0]
    down_split = owned * 5 // 9
    down_all = Merged(slot, [down_one, down_two], [down_split, owned - down_split], [token])
    token = down_all.kept[0]
    slot.start()
    grad_rows = deal_back(deal, returned_grads, width, [token])
    token = grad_rows
    while sum_attn.step < levels:
        for scatter in (sum_one, sum_two, down_all, sum_attn):
            if scatter.step < levels:
                token = scatter.add(slot, [token])
        slot.start()
    every = slice(None)
    unit = w_gate.shape[1] // count
    split = unit * 5 // 9
    places = []
    for which, begin, size in ((0, 0, split), (1, split, unit - split)):
        for part in range(2):
            for i in range(count):
                source = slice(i * size, (i + 1) * size)
                target = slice(i * unit + begin, i * unit + begin + size)
                places.append((which, part, every, source, part, every, target))
    places.append((2, 0, every, every, 2, every, every))
    grad_gate, grad_up, grad_down = finish(
        [sum_one, sum_two, down_all], places, [w_gate.shape, w_up.shape, w_down.shape], [token]
    )
    columns = lambda first, size: slice(first, first + size)
    grad_query, grad_key, grad_value, grad_out = finish(
        [sum_attn],
        [
            (0, 0, every, columns(0, q_width), 0, every, every),
            (0, 0, every, columns(q_width, k_width), 1, every, every),
            (0, 1, every, columns(width, k_width), 2, every, every),
            (0, 1, every, columns(0, width), 3, every, every),
        ],
        [w_query.shape, key_weight.shape, value_weight.shape, w_out.shape],
        [grad_gate],
    )
    small = jnp.sum(returned_grads[:, width:].reshape(count, -1).astype(F32), axis=0)
    small_size = 2 * share_width + 2 * HEAD_SIZE
    small = small[:small_size] + small[small_size : 2 * small_size]
    head_sums = small[2 * share_width : 2 * share_width + 2 * HEAD_SIZE]
    return (
        output_rows,
        grad_rows,
        small[:share_width],
        grad_query,
        grad_key,
        grad_value,
        head_sums[:HEAD_SIZE],
        head_sums[HEAD_SIZE:],
        grad_out,
        small[share_width : 2 * share_width],
        grad_gate,
        grad_up,
        grad_down,
    )


def solution(mesh):
    in_specs = (
        P("dp", None),
        P("dp", None),
        P("dp", None),
        P("dp", None),
        P("dp"),
        P("dp", None),
        P("dp", None),
        P("dp", None),
        P(),
        P(),
        P("dp", None),
        P("dp"),
        P("dp", None),
        P("dp", None),
        P("dp", None),
    )
    out_specs = (
        P("dp", None),
        P("dp", None),
        P("dp"),
        P("dp", None),
        P("dp", None),
        P("dp", None),
        P(),
        P(),
        P("dp", None),
        P("dp"),
        P("dp", None),
        P("dp", None),
        P("dp", None),
    )
    return jax.shard_map(
        per_device, mesh=mesh, in_specs=in_specs, out_specs=out_specs, check_vma=False
    )
```
